32 devices in a mesh: groups: 2 (over y), seq: 16 (over z, x, core).
Axes of the slice: x: 2, y: 2, z: 4, core: 2. Of those that a mesh axis runs over, the one named last changes fastest.
Arguments:
- acts: bfloat16 [256, 2048], P(('groups', 'seq')), parts along dimension 0, may hold values from -6 to 6
- grads: bfloat16 [256, 2048], P(('groups', 'seq')), parts along dimension 0, may hold values from -6 to 6
- basis_in: bfloat16 [2048, 2048], P('seq'), may hold values from -0.125 to 0.125
- basis_out: bfloat16 [2048, 2048], P('seq'), may hold values from -0.125 to 0.125
- eigvals: float32 [2048, 2048], P('seq'), may hold values from 0.02 to 0.5
Outputs:
- preconditioned: bfloat16 [2048, 2, 2048], P('seq', 'groups'), parts along dimension 1
The draws below stay inside these ranges and needn't reach their ends.
There are 2 independent parts, one for each index of `groups`. The reference program is written for one: setup_inputs(seed, part) draws one part's arguments, and reference() takes and returns one part's arrays. A program takes and returns all parts, laid end to end along the dimension named above; an argument that names none is the same for every part. Nothing has to cross between parts.
All inputs are finite; a program needn't handle non-finite values.
Results may differ from the reference program's by a relative error of at most 0.0059.
Values may be sent and summed in bfloat16 or wider, within the bound.
A program may use at most 128 MiB of HBM per device.

```python
import math
import jax
import jax.numpy as jnp
from jax import lax

D = 2048
QLEN = 128
TOKENS = 128


def steps_of(stream_key, dims, split, low, largest):
    factor_of = 1.0
    for axis_at, parts in split:
        heights = jax.random.uniform(jax.random.fold_in(jax.random.fold_in(stream_key, 6), axis_at), (parts,), jnp.float32, low / len(split), largest / len(split))
        factor_of = factor_of * jnp.repeat(jnp.exp(heights), dims[axis_at] // parts).reshape((-1,) + (1,) * (len(dims) - 1 - axis_at))
    return factor_of


def bell_draw(key, extent, spread, reach, pieces=(), dtype=jnp.bfloat16):
    values = spread * jax.random.normal(key, extent, jnp.float32)
    if pieces:
        values = values * steps_of(key, extent, pieces, -0.22, 0.18)
    return jnp.clip(values, -reach, reach).astype(dtype)


def setup_inputs(seed: int = 0, part: int = 0) -> dict:
    streams_of = jax.random.split(jax.random.key(seed), 6)
    own_keys = jax.random.split(jax.random.fold_in(streams_of[5], part), 6)
    return {
        "acts": bell_draw(own_keys[0], (TOKENS, D), 1.0, 6.0, ((0, 16),)),
        "grads": bell_draw(own_keys[1], (TOKENS, D), 1.0, 6.0, ((0, 16),)),
        "basis_in": bell_draw(streams_of[2], (D, D), D ** -0.5, 0.125, ((0, 16),)),
        "basis_out": bell_draw(streams_of[3], (D, D), D ** -0.5, 0.125, ((0, 16),)),
        "eigvals": jnp.clip(jnp.exp(math.log(0.5) - 3.218876 * jax.random.uniform(streams_of[4], (D, D), jnp.float32) ** steps_of(streams_of[4], (D, D), ((0, 16),), -0.2, 0.2)), 0.02, 0.5),
    }


DAMPING = 0.01


def reference(acts, grads, basis_in, basis_out, eigvals):
    rot_in = jnp.dot(acts, basis_in, preferred_element_type=jnp.float32).astype(jnp.bfloat16)
    rot_out = jnp.dot(grads, basis_out, preferred_element_type=jnp.float32).astype(jnp.bfloat16)
    queries = rot_in.shape[0] // QLEN
    in_query = rot_in.reshape(queries, QLEN, D)
    out_query = rot_out.reshape(queries, QLEN, D)
    divisor = QLEN * (eigvals + DAMPING)

    def one_query(pair):
        rotated_in, rotated_out = pair
        raw = jnp.dot(rotated_in.T, rotated_out, preferred_element_type=jnp.float32)
        scaled = (raw / divisor).astype(jnp.bfloat16)
        left = jnp.dot(basis_in, scaled, preferred_element_type=jnp.float32).astype(jnp.bfloat16)
        return jnp.dot(left, basis_out.T, preferred_element_type=jnp.float32).astype(jnp.bfloat16)

    result = lax.map(one_query, (in_query, out_query))
    return jnp.transpose(result, (1, 0, 2))
```

```python
import functools

import jax
import jax.numpy as jnp
from jax import lax
from jax.experimental import pallas as pl
from jax.experimental.pallas import tpu as pltpu
from jax.sharding import PartitionSpec as P

QLEN = 128
DAMPING = 0.01
MESH = pl.DeviceIdType.MESH
F32, BF16 = jnp.float32, jnp.bfloat16


def flip(v, d):
    return 1 - v if d else v


def kernel(ag, bin_, bout, eig, out,
           ag_all, ebf, epan, bpan, binpan, part, rq, zpart, rz, rotq, rin, rout,
           sbuf, left, leftx, psend, precv, ptmp,
           ag_s, ag_r, sl_s, sl_r, q_s, q_r, z_s, z_r, g_s, g_r,
           up_s, dn_s, blk_r, bi_s, bi_r, qy_s, qy_r, ro_s, ro_r, bo_s, bo_r, le_s, le_r, p_s, p_r):
    y = lax.axis_index("groups")
    s = lax.axis_index("seq")
    z, x, c = s // 4, (s // 2) % 2, s % 2
    q = s % 4

    def dev(zz, xx, cc, yy):
        return (yy, zz * 4 + xx * 2 + cc)

    def rc(src, dst, ss, rs, to):
        return pltpu.make_async_remote_copy(
            src_ref=src, dst_ref=dst, send_sem=ss, recv_sem=rs, device_id=to, device_id_type=MESH)

    def arrived(dst, rs):
        rc(dst, dst, rs, rs, dev(z, x, 1 - c, y)).wait_recv()

    def sent(src, ss):
        rc(src, src, ss, ss, dev(z, x, 1 - c, y)).wait_send()

    QP = ((0, 1), (1, 0), (1, 1))

    barrier = pltpu.get_barrier_semaphore()
    for d in range(1, 16):
        pl.semaphore_signal(barrier, inc=1, device_id=(y, (s + d) % 16), device_id_type=MESH)
    for i in range(4):
        pl.semaphore_signal(barrier, inc=1, device_id=(1 - y, z * 4 + i), device_id_type=MESH)
    pl.semaphore_wait(barrier, 19)

    pend = []
    for d in range(1, 16):
        t = (s + d) % 16
        cp = rc(ag.at[:, pl.ds(pl.multiple_of(t * 128, 128), 128)], ag_all.at[s], ag_s.at[d], ag_r.at[16 - d],
                (y, t))
        cp.start()
        pend.append(cp)
    ag_all[s] = ag[:, pl.ds(pl.multiple_of(s * 128, 128), 128)]
    ebf[...] = (1.0 / (QLEN * (eig[...] + DAMPING))).astype(BF16)

    rows = pl.ds(pl.multiple_of(q * 128, 128), 128)
    for i, (dx, dc) in enumerate(QP):
        xx, cc = flip(x, dx), flip(c, dc)
        cols = pl.ds(pl.multiple_of((xx * 4 + cc * 2 + y) * 256, 256), 256)
        for k, (src, dst) in enumerate(((ebf, epan), (bout, bpan.at[0]))):
            cp = rc(src.at[:, cols], dst.at[z, rows], sl_s.at[i, k], sl_r.at[i, k], dev(z, xx, cc, y))
            cp.start()
            pend.append(cp)
    own = pl.ds(pl.multiple_of((q * 2 + y) * 256, 256), 256)
    epan[z, rows] = ebf[:, own]
    bpan[0, z, rows] = bout[:, own]

    for d in range(1, 16):
        arrived(ag_all.at[(s + d) % 16], ag_r.at[d])
    tok = ag_all[...].reshape(256, 128)
    for n in range(4):
        cs = slice(n * 512, n * 512 + 512)
        a = jnp.dot(tok, bin_[:, cs], preferred_element_type=F32).reshape(16, 16, 512)
        part[n, :128] = a[:, :8].reshape(128, 512).astype(BF16)
        b = jnp.dot(tok, bout[:, cs], preferred_element_type=F32).reshape(16, 16, 512)
        part[n, 128:] = b[:, 8:].reshape(128, 512).astype(BF16)
    for i, (dx, dc) in enumerate(QP):
        xx, cc = flip(x, dx), flip(c, dc)
        cp = rc(part.at[xx * 2 + cc], rq.at[i], q_s.at[i], q_r.at[i], dev(z, xx, cc, y))
        cp.start()
        pend.append(cp)

    for i, (dx, dc) in enumerate(QP):
        src = pl.ds(pl.multiple_of((flip(x, dx) * 2 + flip(c, dc)) * 128, 128), 128)
        arrived(epan.at[z, src], sl_r.at[i, 0])
        arrived(bpan.at[0, z, src], sl_r.at[i, 1])

    def hop(j):
        for up, sems in ((True, up_s), (False, dn_s)):
            b = z - j if up else z + j
            ok = (b >= 0) if up else (b <= 3)
            nxt = z + 1 if up else z - 1
            can = (z < 3) if up else (z > 0)
            for k, ref in enumerate((epan, bpan.at[0])):
                if j > 0:
                    @pl.when(ok)
                    def _():
                        arrived(ref.at[b], blk_r.at[b, k])
                if j < 3:
                    @pl.when(ok & can)
                    def _():
                        rc(ref.at[b], ref.at[b], sems.at[j, k], blk_r.at[b, k], dev(nxt, x, c, y)).start()

    def hop_sent():
        for j in range(3):
            for up, sems in ((True, up_s), (False, dn_s)):
                b = z - j if up else z + j
                ok = (b >= 0) if up else (b <= 3)
                can = (z < 3) if up else (z > 0)

                @pl.when(ok & can)
                def _():
                    for k, ref in enumerate((epan, bpan.at[0])):
                        sent(ref.at[b], sems.at[j, k])

    hop(0)

    tot = part[q].astype(F32)
    for i in range(3):
        arrived(rq.at[i], q_r.at[i])
        tot = tot + rq[i].astype(F32)
    for i in range(4):
        zpart[i] = tot[:, i * 128:(i + 1) * 128].astype(BF16)
    for d in range(1, 4):
        zz = (z + d) % 4
        cp = rc(zpart.at[zz], rz.at[4 - d], z_s.at[d], z_r.at[4 - d], dev(zz, x, c, y))
        cp.start()
        pend.append(cp)

    slot = c * 2 + x
    binpan[slot] = bin_[...]
    for i, to in enumerate((dev(z, x, 1 - c, y), dev(z, 1 - x, c, y))):
        cp = rc(bin_, binpan.at[slot], bi_s.at[i], bi_r.at[i], to)
        cp.start()
        pend.append(cp)

    tot = zpart[z].astype(F32)
    for d in range(1, 4):
        arrived(rz.at[d], z_r.at[d])
        tot = tot + rz[d].astype(F32)
    rotq[z] = tot.astype(BF16)
    for d in range(1, 4):
        zz = (z + d) % 4
        cp = rc(rotq.at[z], rotq.at[z], g_s.at[d], g_r.at[4 - d], dev(zz, x, c, y))
        cp.start()
        pend.append(cp)
    hop(1)
    for d in range(1, 4):
        arrived(rotq.at[(z + d) % 4], g_r.at[d])

    rin[y, q] = rotq[:, :128]
    rout[y] = rotq[pl.ds(2 * y, 2), 128:]
    for i in range(1, 8):
        dy, dx, dc = i // 4, (i // 2) % 2, i % 2
        cp = rc(rotq.at[:, pl.ds(0, 128)], rin.at[y, q], qy_s.at[i], qy_r.at[i],
                dev(z, flip(x, dx), flip(c, dc), flip(y, dy)))
        cp.start()
        pend.append(cp)
    cp = rc(rotq.at[pl.ds(2 * (1 - y), 2), pl.ds(128, 128)], rout.at[y], ro_s.at[0], ro_r.at[0],
            dev(z, x, c, 1 - y))
    cp.start()
    pend.append(cp)

    far = c * 2 + 1 - x
    arrived(binpan.at[far], bi_r.at[1])
    cp = rc(binpan.at[far], binpan.at[far], bi_s.at[2], bi_r.at[2], dev(z, x, 1 - c, y))
    cp.start()
    pend.append(cp)

    hop(2)
    hop(3)
    for i, to in ((1, dev(z, x, 1 - c, y)), (2, dev(z, x, c, 1 - y))):
        cp = rc(bpan.at[0], bpan.at[i], bo_s.at[i], bo_r.at[i], to)
        cp.start()
        pend.append(cp)

    for i in range(1, 8):
        dy, dx, dc = i // 4, (i // 2) % 2, i % 2
        arrived(rin.at[flip(y, dy), flip(x, dx) * 2 + flip(c, dc)], qy_r.at[i])
    arrived(rout.at[1 - y], ro_r.at[0])

    for g in range(2):
        ro = jnp.concatenate([rout[g, 0], rout[g, 1]], axis=1)
        for m in range(4):
            for t in range(4):
                raw = lax.dot_general(rin[g, m, t], ro, (((0,), (0,)), ((), ())), preferred_element_type=F32)
                e = epan[m, t * 128:(t + 1) * 128].astype(F32)
                sbuf[m * 512 + t * 128:m * 512 + (t + 1) * 128, g * 256:(g + 1) * 256] = (raw * e).astype(BF16)

    arrived(binpan.at[(1 - c) * 2 + x], bi_r.at[0])
    arrived(binpan.at[(1 - c) * 2 + 1 - x], bi_r.at[2])
    for i in range(4):
        l = jnp.dot(binpan[i], sbuf[...], preferred_element_type=F32).astype(BF16)
        left[0, i] = l[:, :256]
        left[1, i] = l[:, 256:]
    for i in range(1, 4):
        dy, dc = i // 2, i % 2
        yy, cc = flip(y, dy), flip(c, dc)
        cp = rc(left.at[yy, pl.ds(cc * 2, 2)], leftx.at[i], le_s.at[i], le_r.at[i], dev(z, x, cc, yy))
        cp.start()
        pend.append(cp)
    leftx[0] = left[y, pl.ds(c * 2, 2)]

    arrived(bpan.at[2], bo_r.at[2])
    cp = rc(bpan.at[2], bpan.at[3], bo_s.at[3], bo_r.at[3], dev(z, x, 1 - c, y))
    cp.start()
    pend.append(cp)
    arrived(bpan.at[1], bo_r.at[1])
    for i in range(1, 4):
        arrived(leftx.at[i], le_r.at[i])
    arrived(bpan.at[3], bo_r.at[3])

    for n in range(4):
        acc = jnp.zeros((256, 512), F32)
        for i in range(4):
            acc = acc + lax.dot_general(leftx[i].reshape(256, 256), bpan[i, n], (((1,), (1,)), ((), ())),
                                        preferred_element_type=F32)
        ptmp[n] = acc.reshape(2, 128, 512)
        psend[n] = ptmp[n, 1 - x].astype(BF16)
        cp = rc(psend.at[n], precv.at[n], p_s.at[n], p_r.at[n], dev(z, 1 - x, c, y))
        cp.start()
        pend.append(cp)
    for n in range(4):
        arrived(precv.at[n], p_r.at[n])
        out[:, n * 512:(n + 1) * 512] = (ptmp[n, x] + precv[n].astype(F32)).astype(BF16)

    for cp in pend:
        cp.wait_send()
    hop_sent()


def fused(acts, grads, basis_in, basis_out, eigvals):
    ag = jnp.concatenate([acts, grads], axis=0)
    v = pltpu.VMEM
    dma = lambda *n: pltpu.SemaphoreType.DMA(n)
    out = pl.pallas_call(
        kernel,
        out_shape=jax.ShapeDtypeStruct((128, 2048), BF16),
        in_specs=[pl.BlockSpec(memory_space=v)] * 4,
        out_specs=pl.BlockSpec(memory_space=v),
        scratch_shapes=[
            v((16, 16, 128), BF16), v((128, 2048), BF16), v((4, 512, 256), BF16), v((4, 4, 512, 256), BF16),
            v((4, 128, 2048), BF16), v((4, 256, 512), BF16), v((3, 256, 512), BF16), v((4, 256, 128), BF16),
            v((4, 256, 128), BF16), v((4, 256, 128), BF16), v((2, 4, 4, 128, 128), BF16), v((2, 2, 128, 128), BF16),
            v((2048, 512), BF16), v((2, 4, 128, 256), BF16), v((4, 2, 128, 256), BF16),
            v((4, 128, 512), BF16), v((4, 128, 512), BF16), v((4, 2, 128, 512), F32),
            dma(16), dma(16), dma(3, 2), dma(3, 2), dma(3), dma(3), dma(4), dma(4), dma(4), dma(4),
            dma(3, 2), dma(3, 2), dma(4, 2), dma(3), dma(3), dma(8), dma(8), dma(1), dma(1), dma(4), dma(4),
            dma(4), dma(4), dma(4), dma(4),
        ],
        compiler_params=pltpu.CompilerParams(
            collective_id=0, has_side_effects=True, vmem_limit_bytes=48 * 1024 * 1024),
        cost_estimate=pl.CostEstimate(flops=5 * 10**9, bytes_accessed=3 * 10**6, transcendentals=0),
    )(ag, basis_in, basis_out, eigvals)
    return out.reshape(128, 1, 2048)


def body(acts, grads, basis_in, basis_out, eigvals):
    parts = lax.axis_size("seq")
    cols = eigvals.shape[0]
    width = eigvals.shape[1]
    full_in, full_out = (
        lax.all_gather(basis_in, "seq", axis=0, tiled=True),
        lax.all_gather(basis_out, "seq", axis=0, tiled=True),
    )
    rot_in = jnp.dot(acts, full_in, preferred_element_type=jnp.float32).astype(jnp.bfloat16)
    rot_out = jnp.dot(grads, full_out, preferred_element_type=jnp.float32).astype(jnp.bfloat16)
    queries = rot_in.shape[0] * parts // QLEN
    in_cols = lax.all_to_all(rot_in, "seq", split_axis=1, concat_axis=0, tiled=True)
    out_all = lax.all_gather(rot_out, "seq", axis=0, tiled=True)
    raw = jnp.einsum(
        "qlc,qld->cqd",
        in_cols.reshape(queries, QLEN, cols),
        out_all.reshape(queries, QLEN, width),
        preferred_element_type=jnp.float32,
    )
    scaled = (raw / (QLEN * (eigvals[:, None, :] + DAMPING))).astype(jnp.bfloat16)
    by_cols = lax.all_to_all(scaled, "seq", split_axis=2, concat_axis=0, tiled=True)
    left = jnp.dot(
        full_in, by_cols.reshape(width, queries * cols), preferred_element_type=jnp.float32
    )
    left = left.astype(jnp.bfloat16).reshape(width, queries, cols)
    left_rows = lax.all_to_all(left, "seq", split_axis=0, concat_axis=2, tiled=True)
    result = lax.dot_general(
        left_rows.reshape(cols * queries, width),
        full_out,
        (((1,), (1,)), ((), ())),
        preferred_element_type=jnp.float32,
    )
    return result.reshape(cols, queries, width).astype(jnp.bfloat16)


def solution(mesh):
    small = mesh.shape["seq"] == 16 and mesh.shape["groups"] == 2

    def step(acts, *rest):
        return (fused if small and acts.shape == (8, 2048) else body)(acts, *rest)

    return jax.shard_map(
        step,
        mesh=mesh,
        in_specs=(
            P(("groups", "seq"), None),
            P(("groups", "seq"), None),
            P("seq", None),
            P("seq", None),
            P("seq", None),
        ),
        out_specs=P("seq", "groups", None),
        check_vma=False,
    )
```

```python
import functools

import jax
import jax.numpy as jnp
from jax import lax
from jax.experimental import pallas as pl
from jax.experimental.pallas import tpu as pltpu
from jax.sharding import PartitionSpec as P

QLEN = 128
DAMPING = 0.01
MESH = pl.DeviceIdType.MESH
F32, BF16 = jnp.float32, jnp.bfloat16


def flip(v, d):
    return 1 - v if d else v


def kernel(ag, bin_h, bout_h, eig_h, out,
           bin_, bout, eig, ld, ag_all, ebf, epan, bpan, binpan, part, rq, zpart, rz, rotq, rin, rout,
           sbuf, left, leftx, psend, precv, ptmp,
           ag_s, ag_r, sl_s, sl_r, q_s, q_r, z_s, z_r, g_s, g_r,
           up_s, dn_s, blk_r, bi_s, bi_r, qy_s, qy_r, ro_s, ro_r, bo_s, bo_r, le_s, le_r, p_s, p_r):
    y = lax.axis_index("groups")
    s = lax.axis_index("seq")
    z, x, c = s // 4, (s // 2) % 2, s % 2
    q = s % 4

    def dev(zz, xx, cc, yy):
        return (yy, zz * 4 + xx * 2 + cc)

    def rc(src, dst, ss, rs, to):
        return pltpu.make_async_remote_copy(
            src_ref=src, dst_ref=dst, send_sem=ss, recv_sem=rs, device_id=to, device_id_type=MESH)

    def arrived(dst, rs):
        rc(dst, dst, rs, rs, dev(z, x, 1 - c, y)).wait_recv()

    def sent(src, ss):
        rc(src, src, ss, ss, dev(z, x, 1 - c, y)).wait_send()

    QP = ((0, 1), (1, 0), (1, 1))

    loads = [pltpu.make_async_copy(a, b, ld.at[i])
             for i, (a, b) in enumerate(((eig_h, eig), (bout_h, bout), (bin_h, bin_)))]
    for cp in loads:
        cp.start()

    barrier = pltpu.get_barrier_semaphore()
    for d in range(1, 16):
        pl.semaphore_signal(barrier, inc=1, device_id=(y, (s + d) % 16), device_id_type=MESH)
    for i in range(4):
        pl.semaphore_signal(barrier, inc=1, device_id=(1 - y, z * 4 + i), device_id_type=MESH)
    pl.semaphore_wait(barrier, 19)

    pend = []
    for d in range(1, 16):
        t = (s + d) % 16
        cp = rc(ag.at[:, pl.ds(pl.multiple_of(t * 128, 128), 128)], ag_all.at[s], ag_s.at[d], ag_r.at[16 - d],
                (y, t))
        cp.start()
        pend.append(cp)
    ag_all[s] = ag[:, pl.ds(pl.multiple_of(s * 128, 128), 128)]
    for cp in loads:
        cp.wait()
    ebf[...] = (1.0 / (QLEN * (eig[...] + DAMPING))).astype(BF16)

    rows = pl.ds(pl.multiple_of(q * 128, 128), 128)
    for k, (src, dst) in enumerate(((ebf, epan), (bout, bpan.at[0]))):
        for i, (dx, dc) in enumerate(QP):
            xx, cc = flip(x, dx), flip(c, dc)
            cols = pl.ds(pl.multiple_of((xx * 4 + cc * 2 + y) * 256, 256), 256)
            cp = rc(src.at[:, cols], dst.at[z, rows], sl_s.at[i, k], sl_r.at[i, k], dev(z, xx, cc, y))
            cp.start()
            pend.append(cp)
    own = pl.ds(pl.multiple_of((q * 2 + y) * 256, 256), 256)
    epan[z, rows] = ebf[:, own]
    bpan[0, z, rows] = bout[:, own]

    for d in range(1, 16):
        arrived(ag_all.at[(s + d) % 16], ag_r.at[d])
    tok = ag_all[...].reshape(256, 128)
    for n in range(4):
        cs = slice(n * 512, n * 512 + 512)
        a = jnp.dot(tok, bin_[:, cs], preferred_element_type=F32).reshape(16, 16, 512)
        part[n, :128] = a[:, :8].reshape(128, 512).astype(BF16)
        b = jnp.dot(tok, bout[:, cs], preferred_element_type=F32).reshape(16, 16, 512)
        part[n, 128:] = b[:, 8:].reshape(128, 512).astype(BF16)
    for i, (dx, dc) in enumerate(QP):
        xx, cc = flip(x, dx), flip(c, dc)
        cp = rc(part.at[xx * 2 + cc], rq.at[i], q_s.at[i], q_r.at[i], dev(z, xx, cc, y))
        cp.start()
        pend.append(cp)

    for i, (dx, dc) in enumerate(QP):
        src = pl.ds(pl.multiple_of((flip(x, dx) * 2 + flip(c, dc)) * 128, 128), 128)
        arrived(epan.at[z, src], sl_r.at[i, 0])
        arrived(bpan.at[0, z, src], sl_r.at[i, 1])

    pans = (epan, bpan.at[0])

    def share(b):
        for i, to in ((1, dev(z, x, 1 - c, y)), (2, dev(z, x, c, 1 - y))):
            rc(bpan.at[0, b], bpan.at[i, b], bo_s.at[i, b], bo_r.at[i, b], to).start()

    def hop(j, k):
        ref = pans[k]
        for up, sems in ((True, up_s), (False, dn_s)):
            b = z - j if up else z + j
            ok = (b >= 0) if up else (b <= 3)
            nxt = z + 1 if up else z - 1
            can = (z < 3) if up else (z > 0)
            if j > 0:
                @pl.when(ok)
                def _():
                    arrived(ref.at[b], blk_r.at[b, k])
            if j < 3:
                @pl.when(ok & can)
                def _():
                    rc(ref.at[b], ref.at[b], sems.at[j, k], blk_r.at[b, k], dev(nxt, x, c, y)).start()
            if k == 1 and j > 0:
                @pl.when(ok)
                def _():
                    share(b)
        if k == 1 and j == 0:
            share(z)

    def onward(j):
        for up in ((True, False) if j else (True,)):
            b = z - j if up else z + j
            ok = (b >= 0) if up else (b <= 3)

            @pl.when(ok)
            def _():
                arrived(bpan.at[2, b], bo_r.at[2, b])
                rc(bpan.at[2, b], bpan.at[3, b], bo_s.at[3, b], bo_r.at[3, b], dev(z, x, 1 - c, y)).start()

    def hop_sent():
        for j in range(3):
            for up, sems in ((True, up_s), (False, dn_s)):
                b = z - j if up else z + j
                ok = (b >= 0) if up else (b <= 3)
                can = (z < 3) if up else (z > 0)

                @pl.when(ok & can)
                def _():
                    for k in range(2):
                        sent(pans[k].at[b], sems.at[j, k])
        for i in range(1, 4):
            for b in range(4):
                sent(bpan.at[i, b], bo_s.at[i, b])

    hop(0, 0)
    hop(0, 1)

    tot = part[q].astype(F32)
    for i in range(3):
        arrived(rq.at[i], q_r.at[i])
        tot = tot + rq[i].astype(F32)
    for i in range(4):
        zpart[i] = tot[:, i * 128:(i + 1) * 128].astype(BF16)
    for d in range(1, 4):
        zz = (z + d) % 4
        cp = rc(zpart.at[zz], rz.at[4 - d], z_s.at[d], z_r.at[4 - d], dev(zz, x, c, y))
        cp.start()
        pend.append(cp)

    slot = c * 2 + x
    binpan[slot] = bin_[...]
    for i, to in enumerate((dev(z, x, 1 - c, y), dev(z, 1 - x, c, y))):
        cp = rc(bin_, binpan.at[slot], bi_s.at[i], bi_r.at[i], to)
        cp.start()
        pend.append(cp)

    tot = zpart[z].astype(F32)
    for d in range(1, 4):
        arrived(rz.at[d], z_r.at[d])
        tot = tot + rz[d].astype(F32)
    rotq[z] = tot.astype(BF16)
    for d in range(1, 4):
        zz = (z + d) % 4
        cp = rc(rotq.at[z], rotq.at[z], g_s.at[d], g_r.at[4 - d], dev(zz, x, c, y))
        cp.start()
        pend.append(cp)
    hop(1, 0)
    for d in range(1, 4):
        arrived(rotq.at[(z + d) % 4], g_r.at[d])

    rin[y, q] = rotq[:, :128]
    rout[y] = rotq[pl.ds(2 * y, 2), 128:]
    for i in range(1, 8):
        dy, dx, dc = i // 4, (i // 2) % 2, i % 2
        cp = rc(rotq.at[:, pl.ds(0, 128)], rin.at[y, q], qy_s.at[i], qy_r.at[i],
                dev(z, flip(x, dx), flip(c, dc), flip(y, dy)))
        cp.start()
        pend.append(cp)
    cp = rc(rotq.at[pl.ds(2 * (1 - y), 2), pl.ds(128, 128)], rout.at[y], ro_s.at[0], ro_r.at[0],
            dev(z, x, c, 1 - y))
    cp.start()
    pend.append(cp)

    far = c * 2 + 1 - x
    arrived(binpan.at[far], bi_r.at[1])
    cp = rc(binpan.at[far], binpan.at[far], bi_s.at[2], bi_r.at[2], dev(z, x, 1 - c, y))
    cp.start()
    pend.append(cp)

    hop(2, 0)
    hop(1, 1)
    onward(0)
    hop(3, 0)

    for i in range(1, 8):
        dy, dx, dc = i // 4, (i // 2) % 2, i % 2
        arrived(rin.at[flip(y, dy), flip(x, dx) * 2 + flip(c, dc)], qy_r.at[i])
    arrived(rout.at[1 - y], ro_r.at[0])

    for g in range(2):
        ro = jnp.concatenate([rout[g, 0], rout[g, 1]], axis=1)
        for m in range(4):
            for t in range(4):
                raw = lax.dot_general(rin[g, m, t], ro, (((0,), (0,)), ((), ())), preferred_element_type=F32)
                e = epan[m, t * 128:(t + 1) * 128].astype(F32)
                sbuf[m * 512 + t * 128:m * 512 + (t + 1) * 128, g * 256:(g + 1) * 256] = (raw * e).astype(BF16)

    hop(2, 1)
    onward(1)
    arrived(binpan.at[(1 - c) * 2 + x], bi_r.at[0])
    arrived(binpan.at[(1 - c) * 2 + 1 - x], bi_r.at[2])
    for h, xr in enumerate((1 - x, x)):
        for cc in range(2):
            l = jnp.dot(binpan[cc * 2 + xr], sbuf[...], preferred_element_type=F32).astype(BF16)
            left[h, 0, cc] = l[:, :256]
            left[h, 1, cc] = l[:, 256:]
        for i in range(1, 4):
            dy, dc = i // 2, i % 2
            yy, cc = flip(y, dy), flip(c, dc)
            cp = rc(left.at[h, yy, cc], leftx.at[h, i], le_s.at[h, i], le_r.at[h, i], dev(z, x, cc, yy))
            cp.start()
            pend.append(cp)
        leftx[h, 0] = left[h, y, c]
    hop(3, 1)

    def product(h, n):
        acc = jnp.zeros((128, 512), F32)
        for i in range(4):
            acc = acc + lax.dot_general(leftx[h, i], bpan[i, n], (((1,), (1,)), ((), ())),
                                        preferred_element_type=F32)
        return acc

    order = [z, z + 1 - 2 * (z % 2), (z + 2) % 4, 3 - z]
    for i in range(1, 4):
        arrived(leftx.at[0, i], le_r.at[0, i])
    for k, n in enumerate(order):
        if k == 2:
            onward(2)
            onward(3)
        arrived(bpan.at[1, n], bo_r.at[1, n])
        arrived(bpan.at[3, n], bo_r.at[3, n])
        psend[k] = product(0, n).astype(BF16)
        cp = rc(psend.at[k], precv.at[k], p_s.at[k], p_r.at[k], dev(z, 1 - x, c, y))
        cp.start()
        pend.append(cp)
    for i in range(1, 4):
        arrived(leftx.at[1, i], le_r.at[1, i])
    for k, n in enumerate(order):
        ptmp[k] = product(1, n)
    for k, n in enumerate(order):
        arrived(precv.at[k], p_r.at[k])
        out[:, pl.ds(pl.multiple_of(n * 512, 512), 512)] = (ptmp[k] + precv[k].astype(F32)).astype(BF16)

    for cp in pend:
        cp.wait_send()
    hop_sent()


def fused(acts, grads, basis_in, basis_out, eigvals):
    ag = jnp.concatenate([acts, grads], axis=0)
    v = pltpu.VMEM
    dma = lambda *n: pltpu.SemaphoreType.DMA(n)
    out = pl.pallas_call(
        kernel,
        out_shape=jax.ShapeDtypeStruct((128, 2048), BF16),
        in_specs=[pl.BlockSpec(memory_space=v)] + [pl.BlockSpec(memory_space=pltpu.MemorySpace.HBM)] * 3,
        out_specs=pl.BlockSpec(memory_space=v),
        scratch_shapes=[
            v((128, 2048), BF16), v((128, 2048), BF16), v((128, 2048), F32), dma(3),
            v((16, 16, 128), BF16), v((128, 2048), BF16), v((4, 512, 256), BF16), v((4, 4, 512, 256), BF16),
            v((4, 128, 2048), BF16), v((4, 256, 512), BF16), v((3, 256, 512), BF16), v((4, 256, 128), BF16),
            v((4, 256, 128), BF16), v((4, 256, 128), BF16), v((2, 4, 4, 128, 128), BF16), v((2, 2, 128, 128), BF16),
            v((2048, 512), BF16), v((2, 2, 2, 128, 256), BF16), v((2, 4, 128, 256), BF16),
            v((4, 128, 512), BF16), v((4, 128, 512), BF16), v((4, 128, 512), F32),
            dma(16), dma(16), dma(3, 2), dma(3, 2), dma(3), dma(3), dma(4), dma(4), dma(4), dma(4),
            dma(3, 2), dma(3, 2), dma(4, 2), dma(3), dma(3), dma(8), dma(8), dma(1), dma(1), dma(4, 4), dma(4, 4),
            dma(2, 4), dma(2, 4), dma(4), dma(4),
        ],
        compiler_params=pltpu.CompilerParams(
            collective_id=0, has_side_effects=True, vmem_limit_bytes=48 * 1024 * 1024),
        cost_estimate=pl.CostEstimate(flops=5 * 10**9, bytes_accessed=3 * 10**6, transcendentals=0),
    )(ag, basis_in, basis_out, eigvals)
    return out.reshape(128, 1, 2048)


def body(acts, grads, basis_in, basis_out, eigvals):
    parts = lax.axis_size("seq")
    cols = eigvals.shape[0]
    width = eigvals.shape[1]
    full_in, full_out = (
        lax.all_gather(basis_in, "seq", axis=0, tiled=True),
        lax.all_gather(basis_out, "seq", axis=0, tiled=True),
    )
    rot_in = jnp.dot(acts, full_in, preferred_element_type=jnp.float32).astype(jnp.bfloat16)
    rot_out = jnp.dot(grads, full_out, preferred_element_type=jnp.float32).astype(jnp.bfloat16)
    queries = rot_in.shape[0] * parts // QLEN
    in_cols = lax.all_to_all(rot_in, "seq", split_axis=1, concat_axis=0, tiled=True)
    out_all = lax.all_gather(rot_out, "seq", axis=0, tiled=True)
    raw = jnp.einsum(
        "qlc,qld->cqd",
        in_cols.reshape(queries, QLEN, cols),
        out_all.reshape(queries, QLEN, width),
        preferred_element_type=jnp.float32,
    )
    scaled = (raw / (QLEN * (eigvals[:, None, :] + DAMPING))).astype(jnp.bfloat16)
    by_cols = lax.all_to_all(scaled, "seq", split_axis=2, concat_axis=0, tiled=True)
    left = jnp.dot(
        full_in, by_cols.reshape(width, queries * cols), preferred_element_type=jnp.float32
    )
    left = left.astype(jnp.bfloat16).reshape(width, queries, cols)
    left_rows = lax.all_to_all(left, "seq", split_axis=0, concat_axis=2, tiled=True)
    result = lax.dot_general(
        left_rows.reshape(cols * queries, width),
        full_out,
        (((1,), (1,)), ((), ())),
        preferred_element_type=jnp.float32,
    )
    return result.reshape(cols, queries, width).astype(jnp.bfloat16)


def solution(mesh):
    small = mesh.shape["seq"] == 16 and mesh.shape["groups"] == 2

    def step(acts, *rest):
        return (fused if small and acts.shape == (8, 2048) else body)(acts, *rest)

    return jax.shard_map(
        step,
        mesh=mesh,
        in_specs=(
            P(("groups", "seq"), None),
            P(("groups", "seq"), None),
            P("seq", None),
            P("seq", None),
            P("seq", None),
        ),
        out_specs=P("seq", "groups", None),
        check_vma=False,
    )
```

```python
import functools

import jax
import jax.numpy as jnp
from jax import lax
from jax.experimental import pallas as pl
from jax.experimental.pallas import tpu as pltpu
from jax.sharding import PartitionSpec as P

QLEN = 128
DAMPING = 0.01
MESH = pl.DeviceIdType.MESH
F32, BF16 = jnp.float32, jnp.bfloat16


def flip(v, d):
    return 1 - v if d else v


def kernel(ag, bin_h, bout_h, eig_h, out,
           bin_, bout, eig, ld, ag_all, ebf, epan, bpan, binpan, part, rq, zown, zpart, rz, rotq, rin, rout,
           sbuf, left, leftx, psend, precv, ptmp,
           ag_s, ag_r, sl_s, sl_r, q_s, q_r, z_s, z_r, g_s, g_r,
           up_s, dn_s, blk_r, bi_s, bi_r, qy_s, qy_r, ro_s, ro_r, bo_s, bo_r, le_s, le_r, p_s, p_r):
    y = lax.axis_index("groups")
    s = lax.axis_index("seq")
    z, x, c = s // 4, (s // 2) % 2, s % 2
    q = s % 4

    def dev(zz, xx, cc, yy):
        return (yy, zz * 4 + xx * 2 + cc)

    def rc(src, dst, ss, rs, to):
        return pltpu.make_async_remote_copy(
            src_ref=src, dst_ref=dst, send_sem=ss, recv_sem=rs, device_id=to, device_id_type=MESH)

    def arrived(dst, rs):
        rc(dst, dst, rs, rs, dev(z, x, 1 - c, y)).wait_recv()

    def sent(src, ss):
        rc(src, src, ss, ss, dev(z, x, 1 - c, y)).wait_send()

    QP = ((0, 1), (1, 0), (1, 1))

    loads = [pltpu.make_async_copy(a, b, ld.at[i])
             for i, (a, b) in enumerate(((eig_h, eig), (bout_h, bout), (bin_h, bin_)))]
    for cp in loads:
        cp.start()

    barrier = pltpu.get_barrier_semaphore()
    for d in range(1, 16):
        pl.semaphore_signal(barrier, inc=1, device_id=(y, (s + d) % 16), device_id_type=MESH)
    for i in range(4):
        pl.semaphore_signal(barrier, inc=1, device_id=(1 - y, z * 4 + i), device_id_type=MESH)
    pl.semaphore_wait(barrier, 19)

    pend = []
    for d in range(1, 16):
        t = (s + d) % 16
        cp = rc(ag.at[:, pl.ds(pl.multiple_of(t * 128, 128), 128)], ag_all.at[s], ag_s.at[d], ag_r.at[16 - d],
                (y, t))
        cp.start()
        pend.append(cp)
    ag_all[s] = ag[:, pl.ds(pl.multiple_of(s * 128, 128), 128)]
    for cp in loads:
        cp.wait()
    ebf[...] = (1.0 / (QLEN * (eig[...] + DAMPING))).astype(BF16)

    rows = pl.ds(pl.multiple_of(q * 128, 128), 128)

    def slices(k):
        src, dst = ((ebf, epan), (bout, bpan.at[0]))[k]
        for i, (dx, dc) in enumerate(QP):
            xx, cc = flip(x, dx), flip(c, dc)
            cols = pl.ds(pl.multiple_of((xx * 4 + cc * 2 + y) * 256, 256), 256)
            cp = rc(src.at[:, cols], dst.at[z, rows], sl_s.at[i, k], sl_r.at[i, k], dev(z, xx, cc, y))
            cp.start()
            pend.append(cp)

    slices(0)
    own = pl.ds(pl.multiple_of((q * 2 + y) * 256, 256), 256)
    epan[z, rows] = ebf[:, own]
    bpan[0, z, rows] = bout[:, own]

    for d in range(1, 16):
        arrived(ag_all.at[(s + d) % 16], ag_r.at[d])
    tok = ag_all[...].reshape(256, 128)
    for h, basis in enumerate((bin_, bout)):
        for n in range(4):
            a = jnp.dot(tok, basis[:, n * 512:(n + 1) * 512], preferred_element_type=F32).reshape(16, 16, 512)
            part[n, h * 128:(h + 1) * 128] = a[:, h * 8:(h + 1) * 8].reshape(128, 512).astype(BF16)
        half = pl.ds(h * 128, 128)
        for i, (dx, dc) in enumerate(QP):
            xx, cc = flip(x, dx), flip(c, dc)
            cp = rc(part.at[xx * 2 + cc, half], rq.at[i, half], q_s.at[i, h], q_r.at[i, h], dev(z, xx, cc, y))
            cp.start()
            pend.append(cp)
        if h == 0:
            slices(1)

    def slices_in(k):
        for i, (dx, dc) in enumerate(QP):
            src = pl.ds(pl.multiple_of((flip(x, dx) * 2 + flip(c, dc)) * 128, 128), 128)
            arrived(pans[k].at[z, src], sl_r.at[i, k])

    pans = (epan, bpan.at[0])

    def share(b):
        for i, to in ((1, dev(z, x, 1 - c, y)), (2, dev(z, x, c, 1 - y))):
            rc(bpan.at[0, b], bpan.at[i, b], bo_s.at[i, b], bo_r.at[i, b], to).start()

    def hop(j, k):
        ref = pans[k]
        for up, sems in ((True, up_s), (False, dn_s)):
            b = z - j if up else z + j
            ok = (b >= 0) if up else (b <= 3)
            nxt = z + 1 if up else z - 1
            can = (z < 3) if up else (z > 0)
            if j > 0:
                @pl.when(ok)
                def _():
                    arrived(ref.at[b], blk_r.at[b, k])
            if j < 3:
                @pl.when(ok & can)
                def _():
                    rc(ref.at[b], ref.at[b], sems.at[j, k], blk_r.at[b, k], dev(nxt, x, c, y)).start()
            if k == 1 and j > 0:
                @pl.when(ok)
                def _():
                    share(b)
        if k == 1 and j == 0:
            share(z)

    def onward(j):
        for up in ((True, False) if j else (True,)):
            b = z - j if up else z + j
            ok = (b >= 0) if up else (b <= 3)

            @pl.when(ok)
            def _():
                arrived(bpan.at[2, b], bo_r.at[2, b])
                rc(bpan.at[2, b], bpan.at[3, b], bo_s.at[3, b], bo_r.at[3, b], dev(z, x, 1 - c, y)).start()

    def hop_sent():
        for j in range(3):
            for up, sems in ((True, up_s), (False, dn_s)):
                b = z - j if up else z + j
                ok = (b >= 0) if up else (b <= 3)
                can = (z < 3) if up else (z > 0)

                @pl.when(ok & can)
                def _():
                    for k in range(2):
                        sent(pans[k].at[b], sems.at[j, k])
        for i in range(1, 4):
            for b in range(4):
                sent(bpan.at[i, b], bo_s.at[i, b])

    def plane_sum(h):
        half = slice(h * 128, (h + 1) * 128)
        tot = part[q, half].astype(F32)
        for i in range(3):
            arrived(rq.at[i, pl.ds(h * 128, 128)], q_r.at[i, h])
            tot = tot + rq[i, half].astype(F32)
        for i in range(4):
            zown[h, i] = tot[:, i * 128:(i + 1) * 128]
            zpart[h, i] = tot[:, i * 128:(i + 1) * 128].astype(BF16)
        for d in range(1, 4):
            zz = (z + d) % 4
            cp = rc(zpart.at[h, zz], rz.at[h, 4 - d], z_s.at[h, d], z_r.at[h, 4 - d], dev(zz, x, c, y))
            cp.start()
            pend.append(cp)

    def line_sum(h):
        tot = zown[h, z]
        for d in range(1, 4):
            arrived(rz.at[h, d], z_r.at[h, d])
            tot = tot + rz[h, d].astype(F32)
        rotq[h, z] = tot.astype(BF16)
        for d in range(1, 4):
            zz = (z + d) % 4
            cp = rc(rotq.at[h, z], rotq.at[h, z], g_s.at[h, d], g_r.at[h, 4 - d], dev(zz, x, c, y))
            cp.start()
            pend.append(cp)

    FAR = ((1, 0, 1), (2, 1, 0), (3, 1, 1))

    def spread(k):
        b = (z + k) % 4
        rin[y, q, b] = rotq[0, b]
        for i, dy, dx in ((0, 0, 0),) + FAR:
            cp = rc(rotq.at[0, b], rin.at[y, q, b], qy_s.at[i, k], qy_r.at[i, k],
                    dev(z, flip(x, dx), c if i else 1 - c, flip(y, dy)))
            cp.start()
            pend.append(cp)

    def spread_on(k):
        b = (z + k) % 4
        for i, dy, dx in FAR:
            ref = rin.at[flip(y, dy), flip(x, dx) * 2 + c, b]
            arrived(ref, qy_r.at[i, k])
            cp = rc(ref, ref, qy_s.at[3 + i, k], qy_r.at[3 + i, k], dev(z, x, 1 - c, y))
            cp.start()
            pend.append(cp)

    plane_sum(0)
    slices_in(0)
    hop(0, 0)
    plane_sum(1)
    line_sum(0)
    spread(0)
    slices_in(1)
    hop(0, 1)

    slot = c * 2 + x
    binpan[slot] = bin_[...]
    for i, to in enumerate((dev(z, x, 1 - c, y), dev(z, 1 - x, c, y))):
        cp = rc(bin_, binpan.at[slot], bi_s.at[i], bi_r.at[i], to)
        cp.start()
        pend.append(cp)

    line_sum(1)
    for k in range(1, 4):
        arrived(rotq.at[0, (z + k) % 4], g_r.at[0, k])
        spread(k)
    spread_on(0)
    hop(1, 0)
    for k in range(1, 4):
        arrived(rotq.at[1, (z + k) % 4], g_r.at[1, k])
    rout[y] = rotq[1, pl.ds(2 * y, 2)]
    cp = rc(rotq.at[1, pl.ds(2 * (1 - y), 2)], rout.at[y], ro_s.at[0], ro_r.at[0], dev(z, x, c, 1 - y))
    cp.start()
    pend.append(cp)
    for k in range(1, 4):
        spread_on(k)

    far = c * 2 + 1 - x
    arrived(binpan.at[far], bi_r.at[1])
    cp = rc(binpan.at[far], binpan.at[far], bi_s.at[2], bi_r.at[2], dev(z, x, 1 - c, y))
    cp.start()
    pend.append(cp)

    hop(2, 0)
    hop(1, 1)
    onward(0)
    hop(3, 0)

    for k in range(4):
        b = (z + k) % 4
        arrived(rin.at[y, x * 2 + 1 - c, b], qy_r.at[0, k])
        for i, dy, dx in FAR:
            arrived(rin.at[flip(y, dy), flip(x, dx) * 2 + 1 - c, b], qy_r.at[3 + i, k])
    arrived(rout.at[1 - y], ro_r.at[0])

    for g in range(2):
        ro = jnp.concatenate([rout[g, 0], rout[g, 1]], axis=1)
        for m in range(4):
            for t in range(4):
                raw = lax.dot_general(rin[g, m, t], ro, (((0,), (0,)), ((), ())), preferred_element_type=F32)
                e = epan[m, t * 128:(t + 1) * 128].astype(F32)
                sbuf[m * 512 + t * 128:m * 512 + (t + 1) * 128, g * 256:(g + 1) * 256] = (raw * e).astype(BF16)

    hop(2, 1)
    onward(1)
    arrived(binpan.at[(1 - c) * 2 + x], bi_r.at[0])
    arrived(binpan.at[(1 - c) * 2 + 1 - x], bi_r.at[2])
    for h, xr in enumerate((1 - x, x)):
        for cc in range(2):
            l = jnp.dot(binpan[cc * 2 + xr], sbuf[...], preferred_element_type=F32).astype(BF16)
            left[h, 0, cc] = l[:, :256]
            left[h, 1, cc] = l[:, 256:]
        for i in range(1, 4):
            dy, dc = i // 2, i % 2
            yy, cc = flip(y, dy), flip(c, dc)
            cp = rc(left.at[h, yy, cc], leftx.at[h, i], le_s.at[h, i], le_r.at[h, i], dev(z, x, cc, yy))
            cp.start()
            pend.append(cp)
        leftx[h, 0] = left[h, y, c]
    hop(3, 1)

    def product(h, n):
        acc = jnp.zeros((128, 512), F32)
        for i in range(4):
            acc = acc + lax.dot_general(leftx[h, i], bpan[i, n], (((1,), (1,)), ((), ())),
                                        preferred_element_type=F32)
        return acc

    order = [z, z + 1 - 2 * (z % 2), (z + 2) % 4, 3 - z]
    for i in range(1, 4):
        arrived(leftx.at[0, i], le_r.at[0, i])
    for k, n in enumerate(order):
        if k == 2:
            onward(2)
            onward(3)
        arrived(bpan.at[1, n], bo_r.at[1, n])
        arrived(bpan.at[3, n], bo_r.at[3, n])
        psend[k] = product(0, n).astype(BF16)
        cp = rc(psend.at[k], precv.at[k], p_s.at[k], p_r.at[k], dev(z, 1 - x, c, y))
        cp.start()
        pend.append(cp)
    for i in range(1, 4):
        arrived(leftx.at[1, i], le_r.at[1, i])
    for k, n in enumerate(order):
        ptmp[k] = product(1, n)
    for k, n in enumerate(order):
        arrived(precv.at[k], p_r.at[k])
        out[:, pl.ds(pl.multiple_of(n * 512, 512), 512)] = (ptmp[k] + precv[k].astype(F32)).astype(BF16)

    for cp in pend:
        cp.wait_send()
    hop_sent()


def fused(acts, grads, basis_in, basis_out, eigvals):
    ag = jnp.concatenate([acts, grads], axis=0)
    v = pltpu.VMEM
    dma = lambda *n: pltpu.SemaphoreType.DMA(n)
    out = pl.pallas_call(
        kernel,
        out_shape=jax.ShapeDtypeStruct((128, 2048), BF16),
        in_specs=[pl.BlockSpec(memory_space=v)] + [pl.BlockSpec(memory_space=pltpu.MemorySpace.HBM)] * 3,
        out_specs=pl.BlockSpec(memory_space=v),
        scratch_shapes=[
            v((128, 2048), BF16), v((128, 2048), BF16), v((128, 2048), F32), dma(3),
            v((16, 16, 128), BF16), v((128, 2048), BF16), v((4, 512, 256), BF16), v((4, 4, 512, 256), BF16),
            v((4, 128, 2048), BF16), v((4, 256, 512), BF16), v((3, 256, 512), BF16), v((2, 4, 128, 128), F32), v((2, 4, 128, 128), BF16),
            v((2, 4, 128, 128), BF16), v((2, 4, 128, 128), BF16), v((2, 4, 4, 128, 128), BF16), v((2, 2, 128, 128), BF16),
            v((2048, 512), BF16), v((2, 2, 2, 128, 256), BF16), v((2, 4, 128, 256), BF16),
            v((4, 128, 512), BF16), v((4, 128, 512), BF16), v((4, 128, 512), F32),
            dma(16), dma(16), dma(3, 2), dma(3, 2), dma(3, 2), dma(3, 2), dma(2, 4), dma(2, 4), dma(2, 4), dma(2, 4),
            dma(3, 2), dma(3, 2), dma(4, 2), dma(3), dma(3), dma(7, 4), dma(7, 4), dma(1), dma(1), dma(4, 4), dma(4, 4),
            dma(2, 4), dma(2, 4), dma(4), dma(4),
        ],
        compiler_params=pltpu.CompilerParams(
            collective_id=0, has_side_effects=True, vmem_limit_bytes=48 * 1024 * 1024),
        cost_estimate=pl.CostEstimate(flops=5 * 10**9, bytes_accessed=3 * 10**6, transcendentals=0),
    )(ag, basis_in, basis_out, eigvals)
    return out.reshape(128, 1, 2048)


def body(acts, grads, basis_in, basis_out, eigvals):
    parts = lax.axis_size("seq")
    cols = eigvals.shape[0]
    width = eigvals.shape[1]
    full_in, full_out = (
        lax.all_gather(basis_in, "seq", axis=0, tiled=True),
        lax.all_gather(basis_out, "seq", axis=0, tiled=True),
    )
    rot_in = jnp.dot(acts, full_in, preferred_element_type=jnp.float32).astype(jnp.bfloat16)
    rot_out = jnp.dot(grads, full_out, preferred_element_type=jnp.float32).astype(jnp.bfloat16)
    queries = rot_in.shape[0] * parts // QLEN
    in_cols = lax.all_to_all(rot_in, "seq", split_axis=1, concat_axis=0, tiled=True)
    out_all = lax.all_gather(rot_out, "seq", axis=0, tiled=True)
    raw = jnp.einsum(
        "qlc,qld->cqd",
        in_cols.reshape(queries, QLEN, cols),
        out_all.reshape(queries, QLEN, width),
        preferred_element_type=jnp.float32,
    )
    scaled = (raw / (QLEN * (eigvals[:, None, :] + DAMPING))).astype(jnp.bfloat16)
    by_cols = lax.all_to_all(scaled, "seq", split_axis=2, concat_axis=0, tiled=True)
    left = jnp.dot(
        full_in, by_cols.reshape(width, queries * cols), preferred_element_type=jnp.float32
    )
    left = left.astype(jnp.bfloat16).reshape(width, queries, cols)
    left_rows = lax.all_to_all(left, "seq", split_axis=0, concat_axis=2, tiled=True)
    result = lax.dot_general(
        left_rows.reshape(cols * queries, width),
        full_out,
        (((1,), (1,)), ((), ())),
        preferred_element_type=jnp.float32,
    )
    return result.reshape(cols, queries, width).astype(jnp.bfloat16)


def solution(mesh):
    small = mesh.shape["seq"] == 16 and mesh.shape["groups"] == 2

    def step(acts, *rest):
        return (fused if small and acts.shape == (8, 2048) else body)(acts, *rest)

    return jax.shard_map(
        step,
        mesh=mesh,
        in_specs=(
            P(("groups", "seq"), None),
            P(("groups", "seq"), None),
            P("seq", None),
            P("seq", None),
            P("seq", None),
        ),
        out_specs=P("seq", "groups", None),
        check_vma=False,
    )
```

```python
import functools

import jax
import jax.numpy as jnp
from jax import lax
from jax.experimental import pallas as pl
from jax.experimental.pallas import tpu as pltpu
from jax.sharding import PartitionSpec as P

QLEN = 128
DAMPING = 0.01
MESH = pl.DeviceIdType.MESH
F32, BF16 = jnp.float32, jnp.bfloat16


def flip(v, d):
    return 1 - v if d else v


def kernel(ag, bin_h, bout_h, eig_h, out,
           bin_, bout, eig, ld, ag_all, ebf, epan, bpan, binpan, part, rq, zown, zpart, rz, rotq, rin, rout,
           sbuf, left, leftx, psend, precv, ptmp,
           ag_s, ag_r, sl_s, sl_r, q_s, q_r, z_s, z_r, g_s, g_r,
           up_s, dn_s, blk_r, bi_s, bi_r, qy_s, qy_r, ro_s, ro_r, bo_s, bo_r, le_s, le_r, p_s, p_r):
    y = lax.axis_index("groups")
    s = lax.axis_index("seq")
    z, x, c = s // 4, (s // 2) % 2, s % 2
    q = s % 4

    def dev(zz, xx, cc, yy):
        return (yy, zz * 4 + xx * 2 + cc)

    def rc(src, dst, ss, rs, to):
        return pltpu.make_async_remote_copy(
            src_ref=src, dst_ref=dst, send_sem=ss, recv_sem=rs, device_id=to, device_id_type=MESH)

    def arrived(dst, rs):
        rc(dst, dst, rs, rs, dev(z, x, 1 - c, y)).wait_recv()

    def sent(src, ss):
        rc(src, src, ss, ss, dev(z, x, 1 - c, y)).wait_send()

    QP = ((0, 1), (1, 0), (1, 1))

    loads = [pltpu.make_async_copy(a, b, ld.at[i])
             for i, (a, b) in enumerate(((eig_h, eig), (bout_h, bout), (bin_h, bin_)))]
    for cp in loads:
        cp.start()

    barrier = pltpu.get_barrier_semaphore()
    for d in range(1, 16):
        pl.semaphore_signal(barrier, inc=1, device_id=(y, (s + d) % 16), device_id_type=MESH)
    for i in range(4):
        pl.semaphore_signal(barrier, inc=1, device_id=(1 - y, z * 4 + i), device_id_type=MESH)
    pl.semaphore_wait(barrier, 19)

    pend = []
    for d in range(1, 16):
        t = (s + d) % 16
        cp = rc(ag.at[:, pl.ds(pl.multiple_of(t * 128, 128), 128)], ag_all.at[s], ag_s.at[d], ag_r.at[16 - d],
                (y, t))
        cp.start()
        pend.append(cp)
    ag_all[s] = ag[:, pl.ds(pl.multiple_of(s * 128, 128), 128)]
    for cp in loads:
        cp.wait()
    ebf[...] = (1.0 / (QLEN * (eig[...] + DAMPING))).astype(BF16)

    rows = pl.ds(pl.multiple_of(q * 128, 128), 128)

    def slices(k):
        src, dst = ((ebf, epan), (bout, bpan.at[0]))[k]
        for i, (dx, dc) in enumerate(QP):
            xx, cc = flip(x, dx), flip(c, dc)
            cols = pl.ds(pl.multiple_of((xx * 4 + cc * 2 + y) * 256, 256), 256)
            cp = rc(src.at[:, cols], dst.at[z, rows], sl_s.at[i, k], sl_r.at[i, k], dev(z, xx, cc, y))
            cp.start()
            pend.append(cp)

    slices(0)
    own = pl.ds(pl.multiple_of((q * 2 + y) * 256, 256), 256)
    epan[z, rows] = ebf[:, own]
    bpan[0, z, rows] = bout[:, own]

    for d in range(1, 16):
        arrived(ag_all.at[(s + d) % 16], ag_r.at[d])
    tok = ag_all[...].reshape(256, 128)
    for h, basis in enumerate((bin_, bout)):
        for n in range(4):
            a = jnp.dot(tok, basis[:, n * 512:(n + 1) * 512], preferred_element_type=F32).reshape(16, 16, 512)
            part[n, h * 128:(h + 1) * 128] = a[:, h * 8:(h + 1) * 8].reshape(128, 512).astype(BF16)
        half = pl.ds(h * 128, 128)
        for i, (dx, dc) in enumerate(QP):
            xx, cc = flip(x, dx), flip(c, dc)
            cp = rc(part.at[xx * 2 + cc, half], rq.at[i, half], q_s.at[i, h], q_r.at[i, h], dev(z, xx, cc, y))
            cp.start()
            pend.append(cp)
        if h == 0:
            slices(1)

    def slices_in(k):
        for i, (dx, dc) in enumerate(QP):
            src = pl.ds(pl.multiple_of((flip(x, dx) * 2 + flip(c, dc)) * 128, 128), 128)
            arrived(pans[k].at[z, src], sl_r.at[i, k])

    pans = (epan, bpan.at[0])

    def share(b):
        for i, to in ((1, dev(z, x, 1 - c, y)), (2, dev(z, x, c, 1 - y))):
            rc(bpan.at[0, b], bpan.at[i, b], bo_s.at[i, b], bo_r.at[i, b], to).start()

    def hop(j, k):
        ref = pans[k]
        for up, sems in ((True, up_s), (False, dn_s)):
            b = z - j if up else z + j
            ok = (b >= 0) if up else (b <= 3)
            nxt = z + 1 if up else z - 1
            can = (z < 3) if up else (z > 0)
            if j > 0:
                @pl.when(ok)
                def _():
                    arrived(ref.at[b], blk_r.at[b, k])
            if j < 3:
                @pl.when(ok & can)
                def _():
                    rc(ref.at[b], ref.at[b], sems.at[j, k], blk_r.at[b, k], dev(nxt, x, c, y)).start()
            if k == 1 and j > 0:
                @pl.when(ok)
                def _():
                    share(b)
        if k == 1 and j == 0:
            share(z)

    def onward(j):
        for up in ((True, False) if j else (True,)):
            b = z - j if up else z + j
            ok = (b >= 0) if up else (b <= 3)

            @pl.when(ok)
            def _():
                arrived(bpan.at[2, b], bo_r.at[2, b])
                rc(bpan.at[2, b], bpan.at[3, b], bo_s.at[3, b], bo_r.at[3, b], dev(z, x, 1 - c, y)).start()

    def hop_sent():
        for j in range(3):
            for up, sems in ((True, up_s), (False, dn_s)):
                b = z - j if up else z + j
                ok = (b >= 0) if up else (b <= 3)
                can = (z < 3) if up else (z > 0)

                @pl.when(ok & can)
                def _():
                    for k in range(2):
                        sent(pans[k].at[b], sems.at[j, k])
        for i in range(1, 4):
            for b in range(4):
                sent(bpan.at[i, b], bo_s.at[i, b])

    def plane_sum(h):
        half = slice(h * 128, (h + 1) * 128)
        tot = part[q, half].astype(F32)
        for i in range(3):
            arrived(rq.at[i, pl.ds(h * 128, 128)], q_r.at[i, h])
            tot = tot + rq[i, half].astype(F32)
        for i in range(4):
            zown[h, i] = tot[:, i * 128:(i + 1) * 128]
            zpart[h, i] = tot[:, i * 128:(i + 1) * 128].astype(BF16)
        for d in range(1, 4):
            zz = (z + d) % 4
            cp = rc(zpart.at[h, zz], rz.at[h, 4 - d], z_s.at[h, d], z_r.at[h, 4 - d], dev(zz, x, c, y))
            cp.start()
            pend.append(cp)

    def line_sum(h):
        tot = zown[h, z]
        for d in range(1, 4):
            arrived(rz.at[h, d], z_r.at[h, d])
            tot = tot + rz[h, d].astype(F32)
        rotq[h, z] = tot.astype(BF16)
        for d in range(1, 4):
            zz = (z + d) % 4
            cp = rc(rotq.at[h, z], rotq.at[h, z], g_s.at[h, d], g_r.at[h, 4 - d], dev(zz, x, c, y))
            cp.start()
            pend.append(cp)

    FAR = ((1, 0, 1), (2, 1, 0), (3, 1, 1))

    def spread(k):
        b = (z + k) % 4
        rin[y, q, b] = rotq[0, b]
        for i, dy, dx in ((0, 0, 0),) + FAR:
            cp = rc(rotq.at[0, b], rin.at[y, q, b], qy_s.at[i, k], qy_r.at[i, k],
                    dev(z, flip(x, dx), c if i else 1 - c, flip(y, dy)))
            cp.start()
            pend.append(cp)

    def spread_on(k):
        b = (z + k) % 4
        for i, dy, dx in FAR:
            ref = rin.at[flip(y, dy), flip(x, dx) * 2 + c, b]
            arrived(ref, qy_r.at[i, k])
            cp = rc(ref, ref, qy_s.at[3 + i, k], qy_r.at[3 + i, k], dev(z, x, 1 - c, y))
            cp.start()
            pend.append(cp)

    slices_in(0)
    hop(0, 0)
    plane_sum(0)
    slices_in(1)
    hop(0, 1)
    plane_sum(1)
    line_sum(0)
    spread(0)
    hop(1, 0)

    slot = c * 2 + x
    binpan[slot] = bin_[...]
    for i, to in enumerate((dev(z, x, 1 - c, y), dev(z, 1 - x, c, y))):
        cp = rc(bin_, binpan.at[slot], bi_s.at[i], bi_r.at[i], to)
        cp.start()
        pend.append(cp)

    line_sum(1)
    for k in range(1, 4):
        arrived(rotq.at[0, (z + k) % 4], g_r.at[0, k])
        spread(k)
    hop(2, 0)
    hop(1, 1)
    spread_on(0)
    for k in range(1, 4):
        arrived(rotq.at[1, (z + k) % 4], g_r.at[1, k])
    rout[y] = rotq[1, pl.ds(2 * y, 2)]
    cp = rc(rotq.at[1, pl.ds(2 * (1 - y), 2)], rout.at[y], ro_s.at[0], ro_r.at[0], dev(z, x, c, 1 - y))
    cp.start()
    pend.append(cp)
    for k in range(1, 4):
        spread_on(k)

    far = c * 2 + 1 - x
    arrived(binpan.at[far], bi_r.at[1])
    cp = rc(binpan.at[far], binpan.at[far], bi_s.at[2], bi_r.at[2], dev(z, x, 1 - c, y))
    cp.start()
    pend.append(cp)

    onward(0)
    hop(3, 0)

    for k in range(4):
        b = (z + k) % 4
        arrived(rin.at[y, x * 2 + 1 - c, b], qy_r.at[0, k])
        for i, dy, dx in FAR:
            arrived(rin.at[flip(y, dy), flip(x, dx) * 2 + 1 - c, b], qy_r.at[3 + i, k])
    arrived(rout.at[1 - y], ro_r.at[0])

    for g in range(2):
        ro = jnp.concatenate([rout[g, 0], rout[g, 1]], axis=1)
        for m in range(4):
            for t in range(4):
                raw = lax.dot_general(rin[g, m, t], ro, (((0,), (0,)), ((), ())), preferred_element_type=F32)
                e = epan[m, t * 128:(t + 1) * 128].astype(F32)
                sbuf[m * 512 + t * 128:m * 512 + (t + 1) * 128, g * 256:(g + 1) * 256] = (raw * e).astype(BF16)

    hop(2, 1)
    onward(1)
    arrived(binpan.at[(1 - c) * 2 + x], bi_r.at[0])
    arrived(binpan.at[(1 - c) * 2 + 1 - x], bi_r.at[2])
    for h, xr in enumerate((1 - x, x)):
        for cc in range(2):
            l = jnp.dot(binpan[cc * 2 + xr], sbuf[...], preferred_element_type=F32).astype(BF16)
            left[h, 0, cc] = l[:, :256]
            left[h, 1, cc] = l[:, 256:]
        for i in range(1, 4):
            dy, dc = i // 2, i % 2
            yy, cc = flip(y, dy), flip(c, dc)
            cp = rc(left.at[h, yy, cc], leftx.at[h, i], le_s.at[h, i], le_r.at[h, i], dev(z, x, cc, yy))
            cp.start()
            pend.append(cp)
        leftx[h, 0] = left[h, y, c]
    hop(3, 1)

    def product(h, n):
        acc = jnp.zeros((128, 512), F32)
        for i in range(4):
            acc = acc + lax.dot_general(leftx[h, i], bpan[i, n], (((1,), (1,)), ((), ())),
                                        preferred_element_type=F32)
        return acc

    order = [z, z + 1 - 2 * (z % 2), (z + 2) % 4, 3 - z]
    for i in range(1, 4):
        arrived(leftx.at[0, i], le_r.at[0, i])
    for k, n in enumerate(order):
        if k == 2:
            onward(2)
            onward(3)
        arrived(bpan.at[1, n], bo_r.at[1, n])
        arrived(bpan.at[3, n], bo_r.at[3, n])
        psend[k] = product(0, n).astype(BF16)
        cp = rc(psend.at[k], precv.at[k], p_s.at[k], p_r.at[k], dev(z, 1 - x, c, y))
        cp.start()
        pend.append(cp)
    for i in range(1, 4):
        arrived(leftx.at[1, i], le_r.at[1, i])
    for k, n in enumerate(order):
        ptmp[k] = product(1, n)
    for k, n in enumerate(order):
        arrived(precv.at[k], p_r.at[k])
        out[:, pl.ds(pl.multiple_of(n * 512, 512), 512)] = (ptmp[k] + precv[k].astype(F32)).astype(BF16)

    for cp in pend:
        cp.wait_send()
    hop_sent()


def fused(acts, grads, basis_in, basis_out, eigvals):
    ag = jnp.concatenate([acts, grads], axis=0)
    v = pltpu.VMEM
    dma = lambda *n: pltpu.SemaphoreType.DMA(n)
    out = pl.pallas_call(
        kernel,
        out_shape=jax.ShapeDtypeStruct((128, 2048), BF16),
        in_specs=[pl.BlockSpec(memory_space=v)] + [pl.BlockSpec(memory_space=pltpu.MemorySpace.HBM)] * 3,
        out_specs=pl.BlockSpec(memory_space=v),
        scratch_shapes=[
            v((128, 2048), BF16), v((128, 2048), BF16), v((128, 2048), F32), dma(3),
            v((16, 16, 128), BF16), v((128, 2048), BF16), v((4, 512, 256), BF16), v((4, 4, 512, 256), BF16),
            v((4, 128, 2048), BF16), v((4, 256, 512), BF16), v((3, 256, 512), BF16), v((2, 4, 128, 128), F32), v((2, 4, 128, 128), BF16),
            v((2, 4, 128, 128), BF16), v((2, 4, 128, 128), BF16), v((2, 4, 4, 128, 128), BF16), v((2, 2, 128, 128), BF16),
            v((2048, 512), BF16), v((2, 2, 2, 128, 256), BF16), v((2, 4, 128, 256), BF16),
            v((4, 128, 512), BF16), v((4, 128, 512), BF16), v((4, 128, 512), F32),
            dma(16), dma(16), dma(3, 2), dma(3, 2), dma(3, 2), dma(3, 2), dma(2, 4), dma(2, 4), dma(2, 4), dma(2, 4),
            dma(3, 2), dma(3, 2), dma(4, 2), dma(3), dma(3), dma(7, 4), dma(7, 4), dma(1), dma(1), dma(4, 4), dma(4, 4),
            dma(2, 4), dma(2, 4), dma(4), dma(4),
        ],
        compiler_params=pltpu.CompilerParams(
            collective_id=0, has_side_effects=True, vmem_limit_bytes=48 * 1024 * 1024),
        cost_estimate=pl.CostEstimate(flops=5 * 10**9, bytes_accessed=3 * 10**6, transcendentals=0),
    )(ag, basis_in, basis_out, eigvals)
    return out.reshape(128, 1, 2048)


def body(acts, grads, basis_in, basis_out, eigvals):
    parts = lax.axis_size("seq")
    cols = eigvals.shape[0]
    width = eigvals.shape[1]
    full_in, full_out = (
        lax.all_gather(basis_in, "seq", axis=0, tiled=True),
        lax.all_gather(basis_out, "seq", axis=0, tiled=True),
    )
    rot_in = jnp.dot(acts, full_in, preferred_element_type=jnp.float32).astype(jnp.bfloat16)
    rot_out = jnp.dot(grads, full_out, preferred_element_type=jnp.float32).astype(jnp.bfloat16)
    queries = rot_in.shape[0] * parts // QLEN
    in_cols = lax.all_to_all(rot_in, "seq", split_axis=1, concat_axis=0, tiled=True)
    out_all = lax.all_gather(rot_out, "seq", axis=0, tiled=True)
    raw = jnp.einsum(
        "qlc,qld->cqd",
        in_cols.reshape(queries, QLEN, cols),
        out_all.reshape(queries, QLEN, width),
        preferred_element_type=jnp.float32,
    )
    scaled = (raw / (QLEN * (eigvals[:, None, :] + DAMPING))).astype(jnp.bfloat16)
    by_cols = lax.all_to_all(scaled, "seq", split_axis=2, concat_axis=0, tiled=True)
    left = jnp.dot(
        full_in, by_cols.reshape(width, queries * cols), preferred_element_type=jnp.float32
    )
    left = left.astype(jnp.bfloat16).reshape(width, queries, cols)
    left_rows = lax.all_to_all(left, "seq", split_axis=0, concat_axis=2, tiled=True)
    result = lax.dot_general(
        left_rows.reshape(cols * queries, width),
        full_out,
        (((1,), (1,)), ((), ())),
        preferred_element_type=jnp.float32,
    )
    return result.reshape(cols, queries, width).astype(jnp.bfloat16)


def solution(mesh):
    small = mesh.shape["seq"] == 16 and mesh.shape["groups"] == 2

    def step(acts, *rest):
        return (fused if small and acts.shape == (8, 2048) else body)(acts, *rest)

    return jax.shard_map(
        step,
        mesh=mesh,
        in_specs=(
            P(("groups", "seq"), None),
            P(("groups", "seq"), None),
            P("seq", None),
            P("seq", None),
            P("seq", None),
        ),
        out_specs=P("seq", "groups", None),
        check_vma=False,
    )
```
